256 devices in a mesh: rows: 64 (over z, x, core), feat: 4 (over y).
Axes of the slice: x: 4, y: 4, z: 8, core: 2. Of those that a mesh axis runs over, the one named last changes fastest.
Arguments:
- feats: bfloat16 [256, 262144], P('feat', 'rows'), may hold values from -6 to 6
- weight: bfloat16 [256, 256], replicated, may hold values from -0.375 to 0.375
- hub_adj: bfloat16 [262144, 512], P('rows'), may hold values from -0.75 to 0.75
- hub_rows: int32 [512], P('rows'), may hold values from 0 to 4095, as said below
- send_cols: int32 [64, 64, 128], P('rows'), may hold values from 0 to 4095
- send_counts: int32 [64, 64], P('rows'), may hold values from 8 to 128, as said below
- tile_cols: int32 [2048, 4], P('rows'), may hold values from 0 to 63, all different within a row
- tile_vals: bfloat16 [2048, 4, 128, 128], P('rows'), may hold values from -0.25 to 0.25
- cot: bfloat16 [256, 262144], P('feat', 'rows'), may hold values from -6 to 6
Outputs:
- out: bfloat16 [256, 262144], P('feat', 'rows')
- grad_feats: float32 [256, 262144], P('feat', 'rows')
- grad_weight: float32 [256, 256], P(None, 'feat')
The draws below stay inside these ranges and needn't reach their ends.
Inputs may be any that keep to these rules, and one draw needn't show every extreme that they name: `hub_rows`: the 8 entries of one owner are distinct rows of its block. `send_cols`: entries past send_counts are ignored; a list may repeat a row. `send_counts`: in every draw some destination receives 128 rows from every sender. `tile_cols`: the 4 senders of one destination block are distinct.
All inputs are finite; a program needn't handle non-finite values.
Results may differ from the reference program's by a relative error of at most 0.0056.
Values may be sent and summed in bfloat16 or wider, within the bound.
A program may use at most 64 MiB of HBM per device.

```python
import math
import jax
import jax.numpy as jnp
from jax import lax

H = 256
ROWS_DEV = 4096
HUB_DEV = 8
CAP = 128
BLK = 128
TILES = 4
PEERS = 64
NODES = 262144
HUBS = 512
BLOCKS_DEV = 32


def draw_hub_rows(key, part):
    key = jax.random.fold_in(key, 11)
    owner_keys = jax.random.split(key, HUBS // HUB_DEV)

    def choose_rows(owner_key):
        return jax.random.permutation(owner_key, ROWS_DEV)[:HUB_DEV]
    chosen_rows = jax.vmap(choose_rows)(owner_keys)
    return chosen_rows.reshape(-1).astype(jnp.int32)


def draw_send_counts(key, part):
    key = jax.random.fold_in(key, 23)
    count_key, full_key = jax.random.split(key)
    counts = jax.random.randint(count_key, (PEERS, PEERS), max(1, CAP // 16), CAP + 1, dtype=jnp.int32)
    full_dest = jax.random.randint(full_key, (), 0, PEERS, dtype=jnp.int32)
    column = jnp.arange(PEERS, dtype=jnp.int32)[None, :]
    return jnp.where(column == full_dest, CAP, counts).astype(jnp.int32)


def set_ends(drawn, stream_key, least, largest):
    place = [jax.random.randint(jax.random.fold_in(stream_key, axis), (), 0, length) for axis, length in enumerate(drawn.shape)]
    main_axis = drawn.shape.index(max(drawn.shape))
    next_to = place[:main_axis] + [(place[main_axis] + 1) % drawn.shape[main_axis]] + place[main_axis + 1:]
    return drawn.at[tuple(place)].set(least).at[tuple(next_to)].set(largest)


def strengthened(drawn, key, source, target, shards_of, factor):
    def block_of(position):
        return (jnp.arange(drawn.shape[position]) // (drawn.shape[position] // shards_of)).reshape((-1,) + (1,) * (drawn.ndim - 1 - position))

    first = jax.random.permutation(key, shards_of)[block_of(target)]
    other_side = (block_of(target) + shards_of // 2) % shards_of
    return jnp.where((block_of(source) == first) | (block_of(source) == other_side), factor * drawn, drawn)


def levels(own_key, shape, cuts, smallest, top_value):
    gain, own = 1.0, jax.random.fold_in(own_key, 6)
    for position, blocks in cuts:
        draws = jnp.exp(jax.random.uniform(jax.random.fold_in(own, position), (blocks,), jnp.float32, smallest / len(cuts), top_value / len(cuts)))
        gain = gain * jnp.repeat(draws, shape[position] // blocks).reshape([-1 if axis == position else 1 for axis in range(len(shape))])
    return gain


def different_ones(own_key, rows, amount, top, lift):
    ranking = jax.random.permutation(jax.random.fold_in(own_key, 1), amount)
    favour = ranking
    for power in range(3):
        favour = favour * favour // amount
    favour = favour * lift // amount
    lots = jax.random.randint(jax.random.fold_in(own_key, 2), (rows, amount), 0, 4096) + favour
    holders = jax.random.permutation(jax.random.fold_in(own_key, 3), rows)[jnp.arange(amount) % rows]
    lots = jnp.where(jnp.arange(rows)[:, None] == holders[None, :], 1 << 14, lots)
    priority = lots * amount + jnp.arange(amount)
    return lax.top_k(priority.astype(jnp.int32), top)[1].astype(jnp.int32)


def scatter_about(key, extent, width, limit, shards=(), kind=jnp.bfloat16):
    gain = levels(key, extent, shards, -0.22, 0.18) if shards else 1.0
    result = jax.random.normal(key, extent, jnp.float32) * width * gain
    return jnp.minimum(jnp.maximum(result, -limit), limit).astype(kind)


def heavy_noise(own_key, extent, deviation, bound, cuts, heavy, kind=jnp.bfloat16):
    drawn = deviation * jax.random.normal(own_key, extent, jnp.float32)
    if cuts:
        drawn = drawn * levels(own_key, extent, cuts, -0.22, 0.18)
    return jnp.clip(strengthened(drawn, jax.random.fold_in(own_key, 3), *heavy), -bound, bound).astype(kind)


def setup_inputs(seed: int = 0) -> dict:
    arg_keys = jax.random.split(jax.random.key(seed), 10)
    return {
        "feats": scatter_about(arg_keys[0], (H, NODES), 1.0, 6.0, ((0, 4), (1, 64))),
        "weight": scatter_about(arg_keys[1], (H, H), H ** -0.5, 0.375),
        "hub_adj": heavy_noise(arg_keys[2], (NODES, HUBS), HUBS ** -0.5, 0.75, ((0, 64),), (0, 1, 64, 4.0)),
        "hub_rows": draw_hub_rows(jax.random.fold_in(arg_keys[9], 71), 0),
        "send_cols": set_ends(jax.random.randint(arg_keys[4], (PEERS, PEERS, CAP), 0, ROWS_DEV), jax.random.fold_in(arg_keys[4], 1), 0, ROWS_DEV - 1).astype(jnp.int32),
        "send_counts": draw_send_counts(jax.random.fold_in(arg_keys[9], 71), 0),
        "tile_cols": different_ones(arg_keys[6], (PEERS * BLOCKS_DEV), PEERS, TILES, 1024),
        "tile_vals": scatter_about(arg_keys[7], (PEERS * BLOCKS_DEV, TILES, BLK, CAP), (TILES * CAP) ** -0.5, 0.25, ((0, 64),)),
        "cot": scatter_about(arg_keys[8], (H, NODES), 1.0, 6.0, ((0, 4), (1, 64))),
    }


def product(left, right):
    return jnp.dot(left.astype(jnp.float32), right.astype(jnp.float32), precision=lax.Precision.HIGHEST)

def reference(feats, weight, hub_adj, hub_rows, send_cols, send_counts, tile_cols, tile_vals, cot):
    owners = jnp.arange(HUBS, dtype=jnp.int32) // HUB_DEV
    hub_nodes = (owners * ROWS_DEV + hub_rows).astype(jnp.int32)
    hub_feats = feats[:, hub_nodes]
    hub_part = product(hub_feats, hub_adj.T)
    slot_index = jnp.arange(CAP, dtype=jnp.int32)
    live = slot_index[None, None, :] < send_counts[:, :, None]
    sources = (jnp.arange(PEERS, dtype=jnp.int32)[:, None, None] * ROWS_DEV + send_cols).astype(jnp.int32)
    nothing = jnp.zeros((), feats.dtype)

    def gather_dest(dest):
        nodes = jnp.take(sources, dest, axis=1)
        usable = jnp.take(live, dest, axis=1)
        received = jnp.where(usable[None], feats[:, nodes], nothing)
        columns = lax.dynamic_slice_in_dim(tile_cols, dest * BLOCKS_DEV, BLOCKS_DEV, 0)
        values = lax.dynamic_slice_in_dim(tile_vals, dest * BLOCKS_DEV, BLOCKS_DEV, 0)
        picked = received[:, columns]
        summed = jnp.einsum('fbtc,btic->fbi', picked.astype(jnp.float32), values.astype(jnp.float32), precision=lax.Precision.HIGHEST)
        return summed.reshape(H, ROWS_DEV)
    dest_list = jnp.arange(PEERS, dtype=jnp.int32)
    ragged = lax.map(gather_dest, dest_list)
    ragged = jnp.transpose(ragged, (1, 0, 2)).reshape(H, NODES)
    agg = (hub_part + ragged).astype(jnp.bfloat16)
    pre = product(weight.T, agg)
    out = jax.nn.silu(pre).astype(jnp.bfloat16)
    sigma = jax.nn.sigmoid(pre)
    slope = (cot.astype(jnp.float32) * (sigma * (1.0 + pre * (1.0 - sigma)))).astype(jnp.bfloat16)
    grad_weight = product(agg, slope.T) * (1.0 / math.sqrt(NODES))
    grad_agg = product(weight, slope).astype(jnp.bfloat16)
    hub_grad = product(grad_agg, hub_adj)
    grad_feats = jnp.zeros((H, NODES), jnp.float32).at[:, hub_nodes].add(hub_grad)

    def scatter_dest(dest, running):
        block = lax.dynamic_slice_in_dim(grad_agg, dest * ROWS_DEV, ROWS_DEV, 1).reshape(H, BLOCKS_DEV, BLK)
        columns = lax.dynamic_slice_in_dim(tile_cols, dest * BLOCKS_DEV, BLOCKS_DEV, 0)
        values = lax.dynamic_slice_in_dim(tile_vals, dest * BLOCKS_DEV, BLOCKS_DEV, 0)
        per_tile = jnp.einsum('fbi,btic->fbtc', block.astype(jnp.float32), values.astype(jnp.float32), precision=lax.Precision.HIGHEST)
        back = jnp.zeros((H, PEERS, CAP), jnp.float32).at[:, columns].add(per_tile)
        usable = jnp.take(live, dest, axis=1)
        back = jnp.where(usable[None], back, jnp.zeros((), jnp.float32))
        nodes = jnp.take(sources, dest, axis=1)
        return running.at[:, nodes].add(back)
    grad_feats = lax.fori_loop(0, PEERS, scatter_dest, grad_feats)
    return (out, grad_feats, grad_weight)
```

```python
import functools
import math

import jax
import jax.numpy as jnp
from jax import lax
from jax.experimental import pallas as pl
from jax.experimental.pallas import tpu as pltpu
from jax.sharding import PartitionSpec as P

MESH = pl.DeviceIdType.MESH
F32 = jnp.float32
BF16 = jnp.bfloat16
NN = (((1,), (0,)), ((), ()))
NT = (((1,), (1,)), ((), ()))
TN = (((0,), (0,)), ((), ()))
EARLY = 12


def dot(a, b, dims=NN):
    return lax.dot_general(a, b, dims, preferred_element_type=F32)


def layer_kernel(
    feats, weight, hadj_hbm, hubrows, cols, tv_hbm, cot, sm,
    out, gfeats, gweight,
    hadj, tv, feat_hi, onehot_hub, hub_own, hub_z, hub_zb, hub_xc, hub_t, hub_acc,
    send, recv, agg_send, agg_full, cot_full, slopes, outs, gas, ga, chain, bsend, brecv,
    scat, wt, w_y, w_1, w_xc, w_2, w_z, w_3, w_4, h_1, h_xc, h_2, h_z,
    lsem, a_s, a_r, b_s, b_r, hz_s, hz_r, hx_s, hx_r, c_s, c_r, y_s, y_r, g_s, g_r, o_s, o_r,
    wy_s, wy_r, wx_s, wx_r, wz_s, wz_r, w4_s, w4_r, h1_s, h1_r, h2_s, h2_r,
):
    me = lax.axis_index("rows")
    y = lax.axis_index("feat")
    z = lax.div(me, 8)
    xc = lax.rem(me, 8)
    x = lax.div(xc, 2)
    c = lax.rem(xc, 2)

    def dest(k):
        return (
            lax.rem(z + 1 + lax.rem(k, 8), 8) * 8
            + lax.rem(x + 1 + lax.div(k, 16), 4) * 2
            + lax.rem(c + 1 + lax.rem(lax.div(k, 8), 2), 2)
        )

    def source(k):
        return (
            lax.rem(z + 7 - lax.rem(k, 8), 8) * 8
            + lax.rem(x + 3 - lax.div(k, 16), 4) * 2
            + lax.rem(c + 1 + lax.rem(lax.div(k, 8), 2), 2)
        )

    def z_peer(m):
        return lax.rem(z + m, 8)

    def xc_peer(m):
        return lax.rem(xc + m, 8)

    def y_peer(m):
        return lax.rem(y + m, 4)

    def to_rows(src, dst, ssem, rsem, peer):
        return pltpu.make_async_remote_copy(
            src_ref=src, dst_ref=dst, send_sem=ssem, recv_sem=rsem,
            device_id={"rows": peer}, device_id_type=MESH,
        )

    def to_feat(src, dst, ssem, rsem, peer):
        return pltpu.make_async_remote_copy(
            src_ref=src, dst_ref=dst, send_sem=ssem, recv_sem=rsem,
            device_id={"feat": peer}, device_id_type=MESH,
        )

    barrier = pltpu.get_barrier_semaphore()

    @pl.loop(1, 64)
    def _(k):
        pl.semaphore_signal(
            barrier, inc=1, device_id={"rows": lax.rem(me + k, 64)}, device_id_type=MESH
        )

    for m in range(1, 4):
        pl.semaphore_signal(barrier, inc=1, device_id={"feat": y_peer(m)}, device_id_type=MESH)
    load_tv = pltpu.make_async_copy(tv_hbm, tv, lsem.at[0])
    load_hadj = pltpu.make_async_copy(hadj_hbm, hadj, lsem.at[1])
    load_hadj.start()
    load_tv.start()

    for hi in range(8):
        feat_hi[pl.ds(hi * 64, 64), :] = feats[:, pl.ds(hi * 512, 512)]
    row_at = lax.broadcasted_iota(jnp.int32, (16, 4096), 1)
    onehot_hub[...] = jnp.where(row_at == hubrows[...], 1.0, 0.0).astype(BF16)
    own = dot(onehot_hub[...], feats[...], NT)
    hub_own[...] = jnp.concatenate([own[:8], jnp.zeros((8, 64), F32)], axis=1)
    chain[0] = jnp.zeros((64, 128), F32)

    def onehot(col, width):
        low = jnp.broadcast_to(jnp.bitwise_and(col, 511), (512, width))
        at = lax.broadcasted_iota(jnp.int32, (512, width), 0)
        return jnp.where(at == low, 1.0, 0.0).astype(BF16)

    def gather(g):
        p0, p1 = dest(2 * g), dest(2 * g + 1)
        col = jnp.concatenate([cols[pl.ds(p0, 1), :], cols[pl.ds(p1, 1), :]], axis=1)
        picked = dot(feat_hi[...], onehot(col, 256))
        high = jnp.broadcast_to(lax.shift_right_arithmetic(col, 9), (64, 256))
        acc = jnp.zeros((64, 256), F32)
        for hi in range(8):
            acc = jnp.where(high == hi, picked[hi * 64 : hi * 64 + 64], acc)
        acc = acc.astype(BF16)
        send[p0] = acc[:, :128]
        send[p1] = acc[:, 128:]

    def forward(k):
        p = dest(k)
        return to_rows(send.at[p], recv.at[me], a_s.at[p], a_r.at[me], p)

    @pl.loop(0, EARLY)
    def _(g):
        gather(g)

    pl.semaphore_wait(barrier, 66)

    def hub_stage1(m):
        p = z_peer(m)
        return to_rows(hub_own, hub_z.at[z], hz_s.at[p], hz_r.at[z], p * 8 + xc)

    def hub_stage1_in(m):
        p = z_peer(m)
        return to_rows(hub_own, hub_z.at[p], hz_s.at[p], hz_r.at[p], p * 8 + xc)

    @pl.loop(1, 8)
    def _(m):
        hub_stage1(m).start()

    hub_z[z] = hub_own[...]

    @pl.loop(0, 2 * EARLY)
    def _(k):
        forward(k).start()

    def cot_out(m):
        p = y_peer(m)
        return to_feat(
            cot.at[:, pl.ds(pl.multiple_of(p * 1024, 1024), 1024)],
            cot_full.at[pl.ds(pl.multiple_of(y * 64, 64), 64)], c_s.at[p], c_r.at[y], p,
        )

    def cot_in(m):
        p = y_peer(m)
        return to_feat(
            cot.at[:, pl.ds(pl.multiple_of(p * 1024, 1024), 1024)],
            cot_full.at[pl.ds(pl.multiple_of(p * 64, 64), 64)], c_s.at[p], c_r.at[p], p,
        )

    for m in (2, 1, 3):
        cot_out(m).start()
    cot_full[pl.ds(pl.multiple_of(y * 64, 64), 64), :] = cot[
        :, pl.ds(pl.multiple_of(y * 1024, 1024), 1024)
    ]

    @pl.loop(EARLY, 31)
    def _(g):
        gather(g)
        forward(2 * g).start()
        forward(2 * g + 1).start()

    gather(jnp.int32(31))
    forward(jnp.int32(62)).start()
    recv[me] = send[me]

    @pl.loop(1, 8)
    def _(m):
        hub_stage1_in(m).wait_recv()

    hub_zb[...] = hub_z[...].reshape(64, 128).astype(BF16)

    def hub_stage2(m):
        p = xc_peer(m)
        return to_rows(hub_zb, hub_xc.at[xc], hx_s.at[p], hx_r.at[xc], z * 8 + p)

    def hub_stage2_in(m):
        p = xc_peer(m)
        return to_rows(hub_zb, hub_xc.at[p], hx_s.at[p], hx_r.at[p], z * 8 + p)

    @pl.loop(1, 8)
    def _(m):
        hub_stage2(m).start()

    hub_xc[xc] = hub_zb[...]
    load_hadj.wait()
    load_tv.wait()

    @pl.loop(1, 8)
    def _(m):
        hub_stage2_in(m).wait_recv()

    for p in range(8):
        part = hub_xc[p].astype(F32)
        for zz in range(8):
            hub_t[pl.ds(zz * 64 + p * 8, 8), :] = part[zz * 8 : zz * 8 + 8]
    hubs = hub_t[...].T[:64].astype(BF16)

    @pl.loop(0, 8)
    def _(n):
        at = pl.ds(pl.multiple_of(n * 512, 512), 512)
        hub_acc[:, at] = dot(hubs, hadj[at, :], NT)

    @pl.loop(0, 63)
    def _(k):
        q = source(k)
        to_rows(send.at[q], recv.at[q], a_s.at[q], a_r.at[q], q).wait_recv()

    def agg_out(m):
        p = y_peer(m)
        return to_feat(
            agg_send.at[p], agg_full.at[pl.ds(pl.multiple_of(y * 64, 64), 64)],
            y_s.at[p], y_r.at[y], p,
        )

    def agg_in(m):
        p = y_peer(m)
        return to_feat(
            agg_send.at[p], agg_full.at[pl.ds(pl.multiple_of(p * 64, 64), 64)],
            y_s.at[p], y_r.at[p], p,
        )

    for m in (2, 1, 3, 0):
        part = y_peer(m)

        @pl.loop(0, 8)
        def _(i):
            b = part * 8 + i
            acc = hub_acc[:, pl.ds(pl.multiple_of(b * 128, 128), 128)]
            for t in range(4):
                acc = acc + dot(recv[sm[b * 4 + t]], tv[b * 4 + t], NT)
            agg_send[part, :, pl.ds(pl.multiple_of(i * 128, 128), 128)] = acc.astype(BF16)

        if m:
            agg_out(m).start()
    agg_full[pl.ds(pl.multiple_of(y * 64, 64), 64), :] = agg_send[y]
    for m in range(1, 4):
        cot_in(m).wait_recv()
    for m in range(1, 4):
        agg_in(m).wait_recv()

    def ga_out(m, half):
        p = y_peer(m)
        return to_feat(
            gas.at[pl.ds(pl.multiple_of(p * 64, 64), 64), pl.ds(half * 512, 512)],
            ga.at[:, pl.ds(pl.multiple_of(y * 1024 + half * 512, 512), 512)],
            g_s.at[half * 4 + p], g_r.at[half * 4 + y], p,
        )

    def ga_in(m, half):
        p = y_peer(m)
        return to_feat(
            gas.at[pl.ds(pl.multiple_of(p * 64, 64), 64), pl.ds(half * 512, 512)],
            ga.at[:, pl.ds(pl.multiple_of(p * 1024 + half * 512, 512), 512)],
            g_s.at[half * 4 + p], g_r.at[half * 4 + p], p,
        )

    for half in range(2):
        at = pl.ds(half * 512, 512)
        pre = dot(weight[...], agg_full[:, at], TN)
        sigma = jax.nn.sigmoid(pre)
        outs[:, at] = (pre * sigma).astype(BF16)
        slope = (cot_full[:, at].astype(F32) * (sigma * (1.0 + pre * (1.0 - sigma)))).astype(BF16)
        slopes[:, at] = slope
        gas[:, at] = dot(weight[...], slope).astype(BF16)
        for m in (2, 1, 3):
            ga_out(m, half).start()
        ga[:, pl.ds(pl.multiple_of(y * 1024 + half * 512, 512), 512)] = gas[
            pl.ds(pl.multiple_of(y * 64, 64), 64), at
        ]

    for e, m in enumerate((0, 1, 3, 2)):
        part = y_peer(m)
        if m:
            for half in range(2):
                ga_in(m, half).wait_recv()

        @pl.loop(0, 8)
        def _(i):
            b = part * 8 + i
            block = ga[:, pl.ds(pl.multiple_of(b * 128, 128), 128)]
            for t in range(4):
                k = e * 32 + i * 4 + t
                chain[k + 1] = dot(block, tv[b * 4 + t]) + chain[sm[128 + k]]

    def backward(k):
        p = dest(k)
        return to_rows(bsend.at[p], brecv.at[me], b_s.at[p], b_r.at[me], p)

    @pl.loop(0, 63)
    def _(k):
        p = dest(k)
        bsend[p] = chain[sm[256 + p]].astype(BF16)
        backward(k).start()

    brecv[me] = chain[sm[256 + me]].astype(BF16)

    def w_out(m):
        p = y_peer(m)
        return to_feat(
            wt.at[pl.ds(pl.multiple_of(p * 64, 64), 64)], w_y.at[y], wy_s.at[p], wy_r.at[y], p
        )

    def w_in(m):
        p = y_peer(m)
        return to_feat(
            wt.at[pl.ds(pl.multiple_of(p * 64, 64), 64)], w_y.at[p], wy_s.at[p], wy_r.at[p], p
        )

    wt[...] = dot(slopes[...], agg_full[...], NT)
    for m in (2, 1, 3):
        w_out(m).start()
    w_y[y] = wt[pl.ds(pl.multiple_of(y * 64, 64), 64), :]

    def out_out(m):
        p = y_peer(m)
        return to_feat(
            outs.at[pl.ds(pl.multiple_of(p * 64, 64), 64)],
            out.at[:, pl.ds(pl.multiple_of(y * 1024, 1024), 1024)], o_s.at[p], o_r.at[y], p,
        )

    def out_in(m):
        p = y_peer(m)
        return to_feat(
            outs.at[pl.ds(pl.multiple_of(p * 64, 64), 64)],
            out.at[:, pl.ds(pl.multiple_of(p * 1024, 1024), 1024)], o_s.at[p], o_r.at[p], p,
        )

    for m in (2, 1, 3):
        out_out(m).start()
    out[:, pl.ds(pl.multiple_of(y * 1024, 1024), 1024)] = outs[
        pl.ds(pl.multiple_of(y * 64, 64), 64), :
    ]

    terms = dot(ga[...], hadj[...])
    packed = jnp.concatenate([terms[:, :256], terms[:, 256:]], axis=0).T
    for zz in range(4):
        for p in range(8):
            h_1[p, pl.ds(zz * 8, 8), :] = packed[zz * 64 + p * 8 : zz * 64 + p * 8 + 8]

    def h1_out(m):
        p = xc_peer(m)
        return to_rows(h_1.at[p], h_xc.at[xc], h1_s.at[p], h1_r.at[xc], z * 8 + p)

    def h1_in(m):
        p = xc_peer(m)
        return to_rows(h_1.at[p], h_xc.at[p], h1_s.at[p], h1_r.at[p], z * 8 + p)

    @pl.loop(1, 8)
    def _(m):
        h1_out(m).start()

    h_xc[xc] = h_1[xc]

    for m in range(1, 4):
        w_in(m).wait_recv()
    w_1[...] = (w_y[0] + w_y[1] + w_y[2] + w_y[3]).reshape(8, 8, 256)

    def wx_out(m):
        p = xc_peer(m)
        return to_rows(w_1.at[p], w_xc.at[xc], wx_s.at[p], wx_r.at[xc], z * 8 + p)

    def wx_in(m):
        p = xc_peer(m)
        return to_rows(w_1.at[p], w_xc.at[p], wx_s.at[p], wx_r.at[p], z * 8 + p)

    @pl.loop(1, 8)
    def _(m):
        wx_out(m).start()

    w_xc[xc] = w_1[xc]

    def scatter(g):
        q = [source(4 * g + i) for i in range(4)]
        col = jnp.concatenate([cols[pl.ds(p, 1), :] for p in q], axis=1)
        back = jnp.concatenate([brecv[p] for p in q], axis=1).astype(F32)
        high = jnp.broadcast_to(lax.shift_right_arithmetic(col, 9), (64, 512))
        spread = jnp.concatenate(
            [jnp.where(high == hi, back, 0.0).astype(BF16) for hi in range(8)], axis=0
        )
        scat[...] += dot(spread, onehot(col, 512), NT)

    def backward_in(k):
        q = source(k)
        return to_rows(bsend.at[q], brecv.at[q], b_s.at[q], b_r.at[q], q)

    def take(first, last):
        @pl.loop(first, last)
        def _(g):
            for i in range(4):
                backward_in(4 * g + i).wait_recv()
            scatter(g)

    scat[...] = jnp.zeros_like(scat)
    take(0, 2)

    @pl.loop(1, 8)
    def _(m):
        h1_in(m).wait_recv()

    total = h_xc[0]
    for p in range(1, 8):
        total = total + h_xc[p]
    h_2[...] = total.reshape(4, 8, 128)

    def h2_out(m):
        p = z_peer(m)
        return to_rows(h_2.at[lax.rem(p, 4)], h_z.at[z], h2_s.at[p], h2_r.at[z], p * 8 + xc)

    def h2_in(m):
        p = z_peer(m)
        return to_rows(h_2.at[lax.rem(p, 4)], h_z.at[p], h2_s.at[p], h2_r.at[p], p * 8 + xc)

    @pl.loop(1, 8)
    def _(m):
        h2_out(m).start()

    h_z[z] = h_2[lax.rem(z, 4)]

    @pl.loop(1, 8)
    def _(m):
        wx_in(m).wait_recv()

    total = w_xc[0]
    for p in range(1, 8):
        total = total + w_xc[p]
    w_2[...] = total

    def wz_out(m):
        p = z_peer(m)
        return to_rows(w_2, w_z.at[z], wz_s.at[p], wz_r.at[z], p * 8 + xc)

    def wz_in(m):
        p = z_peer(m)
        return to_rows(w_2, w_z.at[p], wz_s.at[p], wz_r.at[p], p * 8 + xc)

    @pl.loop(1, 8)
    def _(m):
        wz_out(m).start()

    w_z[z] = w_2[...]
    take(2, 7)

    @pl.loop(1, 8)
    def _(m):
        wz_in(m).wait_recv()

    total = w_z[0]
    for p in range(1, 8):
        total = total + w_z[p]
    w_3[...] = total

    def w4_out(m):
        p = xc_peer(m)
        return to_rows(w_3, w_4.at[xc], w4_s.at[p], w4_r.at[xc], z * 8 + p)

    def w4_in(m):
        p = xc_peer(m)
        return to_rows(w_3, w_4.at[p], w4_s.at[p], w4_r.at[p], z * 8 + p)

    @pl.loop(1, 8)
    def _(m):
        w4_out(m).start()

    w_4[xc] = w_3[...]

    @pl.loop(1, 8)
    def _(m):
        h2_in(m).wait_recv()

    take(7, 12)

    total = h_z[0]
    for p in range(1, 8):
        total = total + h_z[p]
    hub_grad = jnp.where(jnp.broadcast_to(z, (8, 64)) >= 4, total[:, 64:], total[:, :64])
    coarse = hub_grad.astype(BF16)
    fine = (hub_grad - coarse.astype(F32)).astype(BF16)
    hub16 = jnp.concatenate([coarse.astype(F32), fine.astype(F32)], axis=0).astype(BF16)
    for hi in range(8):
        scat[pl.ds(hi * 64, 64), :] += dot(hub16, onehot_hub[:, pl.ds(hi * 512, 512)], TN)

    @pl.loop(1, 8)
    def _(m):
        w4_in(m).wait_recv()

    gweight[...] = (w_4[...].reshape(64, 256) * (1.0 / math.sqrt(64 * 4096))).T
    for m in range(1, 4):
        out_in(m).wait_recv()

    for m in range(1, 4):
        cot_out(m).wait_send()
        agg_out(m).wait_send()
        ga_out(m, 0).wait_send()
        ga_out(m, 1).wait_send()
        w_out(m).wait_send()
        out_out(m).wait_send()

    @pl.loop(1, 8)
    def _(m):
        hub_stage1(m).wait_send()
        hub_stage2(m).wait_send()
        h1_out(m).wait_send()
        h2_out(m).wait_send()
        wx_out(m).wait_send()
        wz_out(m).wait_send()
        w4_out(m).wait_send()

    @pl.loop(0, 63)
    def _(k):
        forward(k).wait_send()
        backward(k).wait_send()

    take(12, 15)
    for i in range(3):
        backward_in(jnp.int32(60 + i)).wait_recv()
    scatter(jnp.int32(15))
    for hi in range(8):
        gfeats[:, pl.ds(hi * 512, 512)] = scat[pl.ds(hi * 64, 64), :]


def on_device(feats, weight, hub_adj, hub_rows, send_cols, send_counts, tile_cols, tile_vals, cot):
    y = lax.axis_index("feat")
    slot = jnp.arange(128, dtype=jnp.int32)
    cols = jnp.where(slot[None, :] < send_counts[0][:, None], send_cols[0], -1)
    tiles = tile_cols.reshape(128)
    quarter = lax.rem(y + jnp.array([0, 1, 3, 2], jnp.int32), 4)
    worked = tile_cols.reshape(4, 32)[quarter].reshape(128)
    number = slot + 1
    earlier = (worked[None, :] == worked[:, None]) & (slot[None, :] < slot[:, None])
    previous = jnp.max(jnp.where(earlier, number[None, :], 0), axis=1)
    peers = jnp.arange(64, dtype=jnp.int32)
    last = jnp.max(jnp.where(worked[None, :] == peers[:, None], number[None, :], 0), axis=1)
    scalars = jnp.concatenate([tiles, previous, last])
    hubrows = jnp.concatenate([hub_rows, hub_rows]).reshape(16, 1)

    vmem = pl.BlockSpec(memory_space=pltpu.VMEM)
    hbm = pl.BlockSpec(memory_space=pl.ANY)
    smem = pl.BlockSpec(memory_space=pltpu.SMEM)
    dma = lambda n: pltpu.SemaphoreType.DMA((n,))
    out, gfeats, gweight = pl.pallas_call(
        layer_kernel,
        out_shape=(
            jax.ShapeDtypeStruct((64, 4096), BF16),
            jax.ShapeDtypeStruct((64, 4096), F32),
            jax.ShapeDtypeStruct((256, 64), F32),
        ),
        in_specs=[vmem, vmem, hbm, vmem, vmem, hbm, vmem, smem],
        out_specs=(vmem, vmem, vmem),
        scratch_shapes=[
            pltpu.VMEM((4096, 512), BF16),
            pltpu.VMEM((128, 128, 128), BF16),
            pltpu.VMEM((512, 512), BF16),
            pltpu.VMEM((16, 4096), BF16),
            pltpu.VMEM((8, 128), F32),
            pltpu.VMEM((8, 8, 128), F32),
            pltpu.VMEM((64, 128), BF16),
            pltpu.VMEM((8, 64, 128), BF16),
            pltpu.VMEM((512, 128), F32),
            pltpu.VMEM((64, 4096), F32),
            pltpu.VMEM((64, 64, 128), BF16),
            pltpu.VMEM((64, 64, 128), BF16),
            pltpu.VMEM((4, 64, 1024), BF16),
            pltpu.VMEM((256, 1024), BF16),
            pltpu.VMEM((256, 1024), BF16),
            pltpu.VMEM((256, 1024), BF16),
            pltpu.VMEM((256, 1024), BF16),
            pltpu.VMEM((256, 1024), BF16),
            pltpu.VMEM((64, 4096), BF16),
            pltpu.VMEM((129, 64, 128), F32),
            pltpu.VMEM((64, 64, 128), BF16),
            pltpu.VMEM((64, 64, 128), BF16),
            pltpu.VMEM((512, 512), F32),
            pltpu.VMEM((256, 256), F32),
            pltpu.VMEM((4, 64, 256), F32),
            pltpu.VMEM((8, 8, 256), F32),
            pltpu.VMEM((8, 8, 256), F32),
            pltpu.VMEM((8, 256), F32),
            pltpu.VMEM((8, 8, 256), F32),
            pltpu.VMEM((8, 256), F32),
            pltpu.VMEM((8, 8, 256), F32),
            pltpu.VMEM((8, 32, 128), F32),
            pltpu.VMEM((8, 32, 128), F32),
            pltpu.VMEM((4, 8, 128), F32),
            pltpu.VMEM((8, 8, 128), F32),
            dma(2),
            dma(64), dma(64), dma(64), dma(64),
            dma(8), dma(8), dma(8), dma(8),
            dma(4), dma(4), dma(4), dma(4),
            dma(8), dma(8), dma(4), dma(4),
            dma(4), dma(4), dma(8), dma(8), dma(8), dma(8), dma(8), dma(8),
            dma(8), dma(8), dma(8), dma(8),
        ],
        compiler_params=pltpu.CompilerParams(
            collective_id=1, has_side_effects=True, vmem_limit_bytes=48 << 20
        ),
        name="layer",
    )(
        feats, weight, hub_adj, hubrows, cols, tile_vals.reshape(128, 128, 128), cot, scalars,
    )
    return out, gfeats, gweight


def solution(mesh):
    in_specs = (
        P("feat", "rows"),
        P(),
        P("rows", None),
        P("rows"),
        P("rows", None, None),
        P("rows", None),
        P("rows", None),
        P("rows", None, None, None),
        P("feat", "rows"),
    )
    out_specs = (P("feat", "rows"), P("feat", "rows"), P(None, "feat"))
    return jax.shard_map(
        on_device, mesh=mesh, in_specs=in_specs, out_specs=out_specs, check_vma=False
    )
```

```python
import functools
import math

import jax
import jax.numpy as jnp
from jax import lax
from jax.experimental import pallas as pl
from jax.experimental.pallas import tpu as pltpu
from jax.sharding import PartitionSpec as P

MESH = pl.DeviceIdType.MESH
F32 = jnp.float32
BF16 = jnp.bfloat16
NN = (((1,), (0,)), ((), ()))
NT = (((1,), (1,)), ((), ()))
TN = (((0,), (0,)), ((), ()))
ORDER = (0, 1, 3, 2)
FORWARD = ((0, 48), (48, 16))
BACKWARD = ((0, 32), (32, 32))
EARLY = 8


def dot(a, b, dims=NN):
    return lax.dot_general(a, b, dims, preferred_element_type=F32)


def layer_kernel(
    feats_hbm, weight_hbm, hadj_hbm, hub_rows_hbm, cols_hbm, counts_hbm, tiles_hbm, tv_hbm, cot_hbm,
    out_hbm, gfeats_hbm, gweight_hbm,
    feats, weight, cot, cols, hub_rows, counts, tiles, links_v, links,
    hadj, tv, feat_hi, onehot_hub, hub_own, hub_z, hub_zb, hub_xc, hub_t, hub_acc,
    send, recv_0, recv_1, agg_0, agg_1, agg_full, cot_full, slopes, outs, gas, ga, chain_0, chain_1,
    bsend, brecv, out, scat, wt, w_y, w_1, w_xc, w_2, w_z, w_3, w_4, w_5, h_1, h_xc, h_2, h_z,
    lsem, a_s, a_r, b_s, b_r0, b_r, hz_s, hz_r, hx_s, hx_r, c_s, c_r, y_s, y_r, g_s, g_r, o_s, o_r,
    wy_s, wy_r, wx_s, wx_r, wz_s, wz_r, w4_s, w4_r, w5_s, w5_r, h1_s, h1_r, h2_s, h2_r,
):
    agg_send = (agg_0, agg_1)
    chain = (chain_0, chain_1)
    recv = (recv_0, recv_1)
    me = lax.axis_index("rows")
    y = lax.axis_index("feat")
    z = lax.div(me, 8)
    xc = lax.rem(me, 8)
    x = lax.div(xc, 2)
    c = lax.rem(xc, 2)

    def dest(k):
        return (
            lax.rem(z + 1 + lax.rem(k, 8), 8) * 8
            + lax.rem(x + 1 + lax.div(k, 16), 4) * 2
            + lax.rem(c + 1 + lax.rem(lax.div(k, 8), 2), 2)
        )

    def source(k):
        return (
            lax.rem(z + 7 - lax.rem(k, 8), 8) * 8
            + lax.rem(x + 3 - lax.div(k, 16), 4) * 2
            + lax.rem(c + 1 + lax.rem(lax.div(k, 8), 2), 2)
        )

    def z_peer(m):
        return lax.rem(z + m, 8)

    def xc_peer(m):
        return lax.rem(xc + m, 8)

    def y_peer(m):
        return lax.rem(y + m, 4)

    def to_rows(src, dst, ssem, rsem, peer):
        return pltpu.make_async_remote_copy(
            src_ref=src, dst_ref=dst, send_sem=ssem, recv_sem=rsem,
            device_id={"rows": peer}, device_id_type=MESH,
        )

    def to_feat(src, dst, ssem, rsem, peer):
        return pltpu.make_async_remote_copy(
            src_ref=src, dst_ref=dst, send_sem=ssem, recv_sem=rsem,
            device_id={"feat": peer}, device_id_type=MESH,
        )

    loads = [
        pltpu.make_async_copy(a, b, lsem.at[i])
        for i, (a, b) in enumerate((
            (feats_hbm, feats), (cols_hbm, cols), (counts_hbm, counts), (hub_rows_hbm, hub_rows),
            (tiles_hbm, tiles), (cot_hbm, cot), (weight_hbm, weight), (hadj_hbm, hadj), (tv_hbm, tv),
        ))
    ]
    for load in loads:
        load.start()
    barrier = pltpu.get_barrier_semaphore()

    @pl.loop(1, 64)
    def _(k):
        pl.semaphore_signal(
            barrier, inc=1, device_id={"rows": lax.rem(me + k, 64)}, device_id_type=MESH
        )

    for m in range(1, 4):
        pl.semaphore_signal(barrier, inc=1, device_id={"feat": y_peer(m)}, device_id_type=MESH)
    for load in loads[:4]:
        load.wait()

    for hi in range(8):
        feat_hi[pl.ds(hi * 64, 64), :] = feats[:, pl.ds(hi * 512, 512)]
    which = lax.rem(lax.broadcasted_iota(jnp.int32, (16, 128), 0), 8)
    hub_row = jnp.zeros((16, 128), jnp.int32)
    for i in range(8):
        hub_row = jnp.where(which == i, hub_rows[i], hub_row)
    for i in range(32):
        at = lax.broadcasted_iota(jnp.int32, (16, 128), 1) + i * 128
        onehot_hub[:, pl.ds(i * 128, 128)] = jnp.where(at == hub_row, 1.0, 0.0).astype(BF16)
    own = dot(onehot_hub[...], feats[...], NT)
    hub_own[...] = jnp.concatenate([own[:8], jnp.zeros((8, 64), F32)], axis=1)
    for part in range(2):
        chain[part][0] = jnp.zeros(chain[part].shape[1:], F32)

    def onehot(col, width):
        low = jnp.broadcast_to(jnp.bitwise_and(col, 511), (512, width))
        at = lax.broadcasted_iota(jnp.int32, (512, width), 0)
        return jnp.where(at == low, 1.0, 0.0).astype(BF16)

    def live(p):
        slot = lax.broadcasted_iota(jnp.int32, (1, 128), 1)
        return jnp.where(slot < counts[0, p], cols[pl.ds(p, 1), :], -1)

    def gather(g):
        p0, p1 = dest(2 * g), dest(2 * g + 1)
        col = jnp.concatenate([live(p0), live(p1)], axis=1)
        picked = dot(feat_hi[...], onehot(col, 256))
        high = jnp.broadcast_to(lax.shift_right_arithmetic(col, 9), (64, 256))
        acc = jnp.zeros((64, 256), F32)
        for hi in range(8):
            acc = jnp.where(high == hi, picked[hi * 64 : hi * 64 + 64], acc)
        acc = acc.astype(BF16)
        send[p0] = acc[:, :128]
        send[p1] = acc[:, 128:]

    def forward(k, part):
        p = dest(k)
        at = pl.ds(*FORWARD[part])
        return to_rows(send.at[p, at], recv[part].at[me], a_s.at[part], a_r.at[part], p)

    def all_forward(sem, part):
        at = recv[part].at[pl.ds(0, 63)]
        return pltpu.make_async_copy(at, at, sem.at[part])

    def all_backward(sem, buf, part):
        at = buf.at[pl.ds(0, 63), pl.ds(*BACKWARD[part])]
        return pltpu.make_async_copy(at, at, sem.at[part])

    @pl.loop(0, EARLY)
    def _(g):
        gather(g)

    pl.semaphore_wait(barrier, 66)

    def hub_stage1(m):
        p = z_peer(m)
        return to_rows(hub_own, hub_z.at[z], hz_s.at[p], hz_r.at[z], p * 8 + xc)

    def hub_stage1_in(m):
        p = z_peer(m)
        return to_rows(hub_own, hub_z.at[p], hz_s.at[p], hz_r.at[p], p * 8 + xc)

    @pl.loop(1, 8)
    def _(m):
        hub_stage1(m).start()

    hub_z[z] = hub_own[...]

    @pl.loop(0, 2 * EARLY)
    def _(k):
        forward(k, 0).start()

    def cot_out(m):
        p = y_peer(m)
        return to_feat(
            cot.at[:, pl.ds(pl.multiple_of(p * 1024, 1024), 1024)],
            cot_full.at[pl.ds(pl.multiple_of(y * 64, 64), 64)], c_s.at[p], c_r.at[y], p,
        )

    def cot_in(m):
        p = y_peer(m)
        return to_feat(
            cot.at[:, pl.ds(pl.multiple_of(p * 1024, 1024), 1024)],
            cot_full.at[pl.ds(pl.multiple_of(p * 64, 64), 64)], c_s.at[p], c_r.at[p], p,
        )

    loads[5].wait()
    for m in (2, 1, 3):
        cot_out(m).start()
    cot_full[pl.ds(pl.multiple_of(y * 64, 64), 64), :] = cot[
        :, pl.ds(pl.multiple_of(y * 1024, 1024), 1024)
    ]

    @pl.loop(EARLY, 31)
    def _(g):
        gather(g)
        forward(2 * g, 0).start()
        forward(2 * g + 1, 0).start()

    gather(jnp.int32(31))
    forward(jnp.int32(62), 0).start()
    for part in range(2):
        recv[part][me] = send[me, pl.ds(*FORWARD[part]), :]

    @pl.loop(0, 63)
    def _(k):
        forward(k, 1).start()

    @pl.loop(1, 8)
    def _(m):
        hub_stage1_in(m).wait_recv()

    hub_zb[...] = hub_z[...].reshape(64, 128).astype(BF16)

    def hub_stage2(m):
        p = xc_peer(m)
        return to_rows(hub_zb, hub_xc.at[xc], hx_s.at[p], hx_r.at[xc], z * 8 + p)

    def hub_stage2_in(m):
        p = xc_peer(m)
        return to_rows(hub_zb, hub_xc.at[p], hx_s.at[p], hx_r.at[p], z * 8 + p)

    @pl.loop(1, 8)
    def _(m):
        hub_stage2(m).start()

    hub_xc[xc] = hub_zb[...]

    loads[4].wait()
    lane = lax.broadcasted_iota(jnp.int32, (1, 128), 1)
    senders = jnp.zeros((1, 128), jnp.int32)
    for e, m in enumerate(ORDER):
        first = y_peer(m) * 8

        def add(i, row):
            for t in range(4):
                row = jnp.where(lane == e * 32 + i * 4 + t, tiles[first + i, t], row)
            return row

        senders = lax.fori_loop(0, 8, add, senders)
    across = jnp.broadcast_to(senders, (128, 128))
    down = across.T
    at_row = lax.broadcasted_iota(jnp.int32, (128, 128), 0)
    at_lane = lax.broadcasted_iota(jnp.int32, (128, 128), 1)
    before = jnp.where(at_row < at_lane, jnp.where(across == down, at_row + 1, 0), 0)
    final = jnp.where(down == at_lane, at_row + 1, 0)
    links_v[...] = jnp.concatenate([
        jnp.max(before, axis=0, keepdims=True), jnp.max(final, axis=0, keepdims=True),
        jnp.zeros((6, 128), jnp.int32),
    ], axis=0)
    fetch = pltpu.make_async_copy(links_v, links, lsem.at[9])
    fetch.start()
    fetch.wait()
    for load in loads[6:]:
        load.wait()

    @pl.loop(1, 8)
    def _(m):
        hub_stage2_in(m).wait_recv()

    for p in range(8):
        part = hub_xc[p].astype(F32)
        for zz in range(8):
            hub_t[pl.ds(zz * 64 + p * 8, 8), :] = part[zz * 8 : zz * 8 + 8]
    hubs = hub_t[...].T[:64].astype(BF16)

    @pl.loop(0, 8)
    def _(n):
        at = pl.ds(pl.multiple_of(n * 512, 512), 512)
        hub_acc[:, at] = dot(hubs, hadj[at, :], NT)

    def agg_move(m, part, slot):
        p = y_peer(m)
        first, count = FORWARD[part]
        return to_feat(
            agg_send[part].at[p],
            agg_full.at[pl.ds(pl.multiple_of(slot * 64 + first, 16), count)],
            y_s.at[part * 4 + p], y_r.at[part * 4 + slot], p,
        )

    def agg_out(m, part):
        return agg_move(m, part, y)

    def agg_in(m, part):
        return agg_move(m, part, y_peer(m))

    def block_tiles(b):
        return jnp.concatenate([tv[b * 4 + t] for t in range(4)], axis=1)

    for part in range(2):
        first, count = FORWARD[part]
        rows = pl.ds(first, count)
        all_forward(a_r, part).wait()
        for m in (2, 1, 3, 0):
            quarter = y_peer(m)

            @pl.loop(0, 8)
            def _(i):
                b = quarter * 8 + i
                listed = jnp.concatenate(
                    [recv[part][tiles[b, t]] for t in range(4)], axis=1
                )
                acc = hub_acc[rows, pl.ds(pl.multiple_of(b * 128, 128), 128)]
                acc = acc + dot(listed, block_tiles(b), NT)
                agg_send[part][quarter, :, pl.ds(pl.multiple_of(i * 128, 128), 128)] = acc.astype(
                    BF16
                )

            if m:
                agg_out(m, part).start()
        agg_full[pl.ds(pl.multiple_of(y * 64 + first, 16), count), :] = agg_send[part][y]
    for m in range(1, 4):
        cot_in(m).wait_recv()
    for part in range(2):
        for m in range(1, 4):
            agg_in(m, part).wait_recv()

    def ga_move(m, part, half, slot):
        p = y_peer(m)
        first, count = BACKWARD[part]
        sem = part * 8 + half * 4
        return to_feat(
            gas.at[pl.ds(pl.multiple_of(p * 64 + first, 16), count), pl.ds(half * 512, 512)],
            ga.at[
                pl.ds(first, count), pl.ds(pl.multiple_of(slot * 1024 + half * 512, 512), 512)
            ],
            g_s.at[sem + p], g_r.at[sem + slot], p,
        )

    def ga_out(m, part, half):
        return ga_move(m, part, half, y)

    def ga_in(m, part, half):
        return ga_move(m, part, half, y_peer(m))

    for half in range(2):
        at = pl.ds(half * 512, 512)
        pre = dot(weight[...], agg_full[:, at], TN)
        sigma = jax.nn.sigmoid(pre)
        outs[:, at] = (pre * sigma).astype(BF16)
        slope = (cot_full[:, at].astype(F32) * (sigma * (1.0 + pre * (1.0 - sigma)))).astype(BF16)
        slopes[:, at] = slope
        gas[:, at] = dot(weight[...], slope).astype(BF16)
        for m in (2, 1, 3):
            ga_out(m, 0, half).start()
        ga[:, pl.ds(pl.multiple_of(y * 1024 + half * 512, 512), 512)] = gas[
            pl.ds(pl.multiple_of(y * 64, 64), 64), at
        ]
    for half in range(2):
        for m in (2, 1, 3):
            ga_out(m, 1, half).start()

    def w_out(m):
        p = y_peer(m)
        return to_feat(
            wt.at[pl.ds(pl.multiple_of(p * 64, 64), 64)], w_y.at[y], wy_s.at[p], wy_r.at[y], p
        )

    def w_in(m):
        p = y_peer(m)
        return to_feat(
            wt.at[pl.ds(pl.multiple_of(p * 64, 64), 64)], w_y.at[p], wy_s.at[p], wy_r.at[p], p
        )

    wt[...] = dot(slopes[...], agg_full[...], NT)
    for m in (2, 1, 3):
        w_out(m).start()
    w_y[y] = wt[pl.ds(pl.multiple_of(y * 64, 64), 64), :]

    def out_out(m):
        p = y_peer(m)
        return to_feat(
            outs.at[pl.ds(pl.multiple_of(p * 64, 64), 64)],
            out.at[:, pl.ds(pl.multiple_of(y * 1024, 1024), 1024)], o_s.at[p], o_r.at[y], p,
        )

    def out_in(m):
        p = y_peer(m)
        return to_feat(
            outs.at[pl.ds(pl.multiple_of(p * 64, 64), 64)],
            out.at[:, pl.ds(pl.multiple_of(p * 1024, 1024), 1024)], o_s.at[p], o_r.at[p], p,
        )

    for m in (2, 1, 3):
        out_out(m).start()
    out[:, pl.ds(pl.multiple_of(y * 1024, 1024), 1024)] = outs[
        pl.ds(pl.multiple_of(y * 64, 64), 64), :
    ]

    def backward(k, part):
        p = dest(k)
        at = pl.ds(*BACKWARD[part])
        rsem = b_r.at[me] if part else b_r0.at[0]
        return to_rows(bsend.at[p, at], brecv.at[me, at], b_s.at[part], rsem, p)

    def tile_products(part):
        first, count = BACKWARD[part]
        for e, m in enumerate(ORDER):
            quarter = y_peer(m)
            if m:
                for half in range(2):
                    ga_in(m, part, half).wait_recv()

            @pl.loop(0, 8)
            def _(i):
                b = quarter * 8 + i
                block = ga[pl.ds(first, count), pl.ds(pl.multiple_of(b * 128, 128), 128)]
                products = dot(block, block_tiles(b))
                for t in range(4):
                    k = e * 32 + i * 4 + t
                    chain[part][k + 1] = (
                        products[:, t * 128 : t * 128 + 128] + chain[part][links[0, k]]
                    )

    def send_back(part):
        first, count = BACKWARD[part]

        @pl.loop(0, 63)
        def _(k):
            p = dest(k)
            bsend[p, pl.ds(first, count), :] = chain[part][links[1, p]].astype(BF16)
            backward(k, part).start()

        brecv[me, pl.ds(first, count), :] = chain[part][links[1, me]].astype(BF16)

    tile_products(0)
    send_back(0)
    tile_products(1)
    terms = dot(ga[...], hadj[...])
    packed = jnp.concatenate([terms[:, :256], terms[:, 256:]], axis=0).T
    for zz in range(4):
        for p in range(8):
            h_1[p, pl.ds(zz * 8, 8), :] = packed[zz * 64 + p * 8 : zz * 64 + p * 8 + 8]

    def h1_out(m):
        p = xc_peer(m)
        return to_rows(h_1.at[p], h_xc.at[xc], h1_s.at[p], h1_r.at[xc], z * 8 + p)

    def h1_in(m):
        p = xc_peer(m)
        return to_rows(h_1.at[p], h_xc.at[p], h1_s.at[p], h1_r.at[p], z * 8 + p)

    @pl.loop(1, 8)
    def _(m):
        h1_out(m).start()

    h_xc[xc] = h_1[xc]

    for m in range(1, 4):
        w_in(m).wait_recv()
    w_1[...] = (w_y[0] + w_y[1] + w_y[2] + w_y[3]).reshape(8, 8, 256)

    def wx_out(m):
        p = xc_peer(m)
        return to_rows(w_1.at[p], w_xc.at[xc], wx_s.at[p], wx_r.at[xc], z * 8 + p)

    def wx_in(m):
        p = xc_peer(m)
        return to_rows(w_1.at[p], w_xc.at[p], wx_s.at[p], wx_r.at[p], z * 8 + p)

    @pl.loop(1, 8)
    def _(m):
        wx_out(m).start()

    w_xc[xc] = w_1[xc]

    send_back(1)

    def scatter(g):
        q = [source(4 * g + i) for i in range(4)]
        col = jnp.concatenate([live(p) for p in q], axis=1)
        back = jnp.concatenate([brecv[p] for p in q], axis=1).astype(F32)
        high = jnp.broadcast_to(lax.shift_right_arithmetic(col, 9), (64, 512))
        spread = jnp.concatenate(
            [jnp.where(high == hi, back, 0.0).astype(BF16) for hi in range(8)], axis=0
        )
        scat[...] += dot(spread, onehot(col, 512), NT)

    def backward_in(k):
        q = source(k)
        at = pl.ds(*BACKWARD[1])
        return to_rows(bsend.at[q, at], brecv.at[q, at], b_s.at[1], b_r.at[q], q)

    def take(first, last):
        @pl.loop(first, last)
        def _(g):
            for i in range(4):
                backward_in(4 * g + i).wait_recv()
            scatter(g)

    scat[...] = jnp.zeros_like(scat)

    @pl.loop(1, 8)
    def _(m):
        h1_in(m).wait_recv()

    total = h_xc[0]
    for p in range(1, 8):
        total = total + h_xc[p]
    h_2[...] = total.reshape(4, 8, 128)

    def h2_out(m):
        p = z_peer(m)
        return to_rows(h_2.at[lax.rem(p, 4)], h_z.at[z], h2_s.at[p], h2_r.at[z], p * 8 + xc)

    def h2_in(m):
        p = z_peer(m)
        return to_rows(h_2.at[lax.rem(p, 4)], h_z.at[p], h2_s.at[p], h2_r.at[p], p * 8 + xc)

    @pl.loop(1, 8)
    def _(m):
        h2_out(m).start()

    h_z[z] = h_2[lax.rem(z, 4)]

    @pl.loop(1, 8)
    def _(m):
        wx_in(m).wait_recv()

    total = w_xc[0]
    for p in range(1, 8):
        total = total + w_xc[p]
    for i in range(8):
        w_2[i] = total[i : i + 1]

    def wz_out(m):
        p = z_peer(m)
        return to_rows(w_2.at[p], w_z.at[z], wz_s.at[p], wz_r.at[z], p * 8 + xc)

    def wz_in(m):
        p = z_peer(m)
        return to_rows(w_2.at[p], w_z.at[p], wz_s.at[p], wz_r.at[p], p * 8 + xc)

    @pl.loop(1, 8)
    def _(m):
        wz_out(m).start()

    w_z[z] = w_2[z]
    all_backward(b_r0, brecv, 0).wait()
    take(0, 4)

    @pl.loop(1, 8)
    def _(m):
        wz_in(m).wait_recv()

    total = w_z[0]
    for p in range(1, 8):
        total = total + w_z[p]
    w_3[...] = total

    def w4_out(m):
        p = z_peer(m)
        return to_rows(w_3, w_4.at[z], w4_s.at[p], w4_r.at[z], p * 8 + xc)

    def w4_in(m):
        p = z_peer(m)
        return to_rows(w_3, w_4.at[p], w4_s.at[p], w4_r.at[p], p * 8 + xc)

    @pl.loop(1, 8)
    def _(m):
        w4_out(m).start()

    w_4[z] = w_3[...]

    @pl.loop(1, 8)
    def _(m):
        h2_in(m).wait_recv()

    take(4, 8)

    @pl.loop(1, 8)
    def _(m):
        w4_in(m).wait_recv()

    def w5_out(m):
        p = xc_peer(m)
        return to_rows(w_4, w_5.at[xc], w5_s.at[p], w5_r.at[xc], z * 8 + p)

    def w5_in(m):
        p = xc_peer(m)
        return to_rows(w_4, w_5.at[p], w5_s.at[p], w5_r.at[p], z * 8 + p)

    @pl.loop(1, 8)
    def _(m):
        w5_out(m).start()

    w_5[xc] = w_4[...]
    take(8, 12)

    total = h_z[0]
    for p in range(1, 8):
        total = total + h_z[p]
    hub_grad = jnp.where(jnp.broadcast_to(z, (8, 64)) >= 4, total[:, 64:], total[:, :64])
    coarse = hub_grad.astype(BF16)
    fine = (hub_grad - coarse.astype(F32)).astype(BF16)
    hub16 = jnp.concatenate([coarse.astype(F32), fine.astype(F32)], axis=0).astype(BF16)
    for hi in range(8):
        scat[pl.ds(hi * 64, 64), :] += dot(hub16, onehot_hub[:, pl.ds(hi * 512, 512)], TN)

    @pl.loop(1, 8)
    def _(m):
        w5_in(m).wait_recv()

    for m in range(1, 4):
        out_in(m).wait_recv()
    stores = [
        pltpu.make_async_copy(out, out_hbm, lsem.at[0]),
        pltpu.make_async_copy(w_5, gweight_hbm, lsem.at[1]),
    ]
    for store in stores:
        store.start()

    for m in range(1, 4):
        cot_out(m).wait_send()
        for part in range(2):
            agg_out(m, part).wait_send()
            ga_out(m, part, 0).wait_send()
            ga_out(m, part, 1).wait_send()
        w_out(m).wait_send()
        out_out(m).wait_send()

    @pl.loop(1, 8)
    def _(m):
        hub_stage1(m).wait_send()
        hub_stage2(m).wait_send()
        h1_out(m).wait_send()
        h2_out(m).wait_send()
        wx_out(m).wait_send()
        wz_out(m).wait_send()
        w4_out(m).wait_send()
        w5_out(m).wait_send()

    for part in range(2):
        all_forward(a_s, part).wait()
    take(12, 15)
    for i in range(3):
        backward_in(jnp.int32(60 + i)).wait_recv()
    scatter(jnp.int32(15))
    for hi in range(8):
        store = pltpu.make_async_copy(
            scat.at[pl.ds(hi * 64, 64)], gfeats_hbm.at[:, pl.ds(hi * 512, 512)], lsem.at[2 + hi]
        )
        store.start()
        stores.append(store)
    for part in range(2):
        all_backward(b_s, bsend, part).wait()
    for store in stores:
        store.wait()


def on_device(feats, weight, hub_adj, hub_rows, send_cols, send_counts, tile_cols, tile_vals, cot):
    hbm = pl.BlockSpec(memory_space=pl.ANY)
    vmem = pltpu.VMEM
    dma = lambda n: pltpu.SemaphoreType.DMA((n,))
    out, gfeats, gweight = pl.pallas_call(
        layer_kernel,
        out_shape=(
            jax.ShapeDtypeStruct((64, 4096), BF16),
            jax.ShapeDtypeStruct((64, 4096), F32),
            jax.ShapeDtypeStruct((8, 8, 1, 256), F32),
        ),
        in_specs=[hbm] * 9,
        out_specs=(hbm,) * 3,
        scratch_shapes=[
            vmem((64, 4096), BF16),
            vmem((256, 256), BF16),
            vmem((64, 4096), BF16),
            vmem((64, 128), jnp.int32),
            pltpu.SMEM((8,), jnp.int32),
            pltpu.SMEM((1, 64), jnp.int32),
            pltpu.SMEM((32, 4), jnp.int32),
            vmem((8, 128), jnp.int32),
            pltpu.SMEM((8, 128), jnp.int32),
            vmem((4096, 512), BF16),
            vmem((128, 128, 128), BF16),
            vmem((512, 512), BF16),
            vmem((16, 4096), BF16),
            vmem((8, 128), F32),
            vmem((8, 8, 128), F32),
            vmem((64, 128), BF16),
            vmem((8, 64, 128), BF16),
            vmem((512, 128), F32),
            vmem((64, 4096), F32),
            vmem((64, 64, 128), BF16),
            vmem((64, FORWARD[0][1], 128), BF16),
            vmem((64, FORWARD[1][1], 128), BF16),
            vmem((4, FORWARD[0][1], 1024), BF16),
            vmem((4, FORWARD[1][1], 1024), BF16),
            vmem((256, 1024), BF16),
            vmem((256, 1024), BF16),
            vmem((256, 1024), BF16),
            vmem((256, 1024), BF16),
            vmem((256, 1024), BF16),
            vmem((64, 4096), BF16),
            vmem((129, BACKWARD[0][1], 128), F32),
            vmem((129, BACKWARD[1][1], 128), F32),
            vmem((64, 64, 128), BF16),
            vmem((64, 64, 128), BF16),
            vmem((64, 4096), BF16),
            vmem((512, 512), F32),
            vmem((256, 256), F32),
            vmem((4, 64, 256), F32),
            vmem((8, 8, 256), F32),
            vmem((8, 8, 256), F32),
            vmem((8, 1, 256), F32),
            vmem((8, 1, 256), F32),
            vmem((1, 256), F32),
            vmem((8, 1, 256), F32),
            vmem((8, 8, 1, 256), F32),
            vmem((8, 32, 128), F32),
            vmem((8, 32, 128), F32),
            vmem((4, 8, 128), F32),
            vmem((8, 8, 128), F32),
            dma(10),
            dma(2), dma(2), dma(2), dma(1), dma(64),
            dma(8), dma(8), dma(8), dma(8),
            dma(4), dma(4), dma(8), dma(8),
            dma(16), dma(16), dma(4), dma(4),
            dma(4), dma(4), dma(8), dma(8), dma(8), dma(8),
            dma(8), dma(8), dma(8), dma(8),
            dma(8), dma(8), dma(8), dma(8),
        ],
        compiler_params=pltpu.CompilerParams(
            collective_id=1, has_side_effects=True, vmem_limit_bytes=60 << 20
        ),
        name="layer",
    )(
        feats, weight, hub_adj, hub_rows, send_cols.reshape(64, 128), send_counts, tile_cols,
        tile_vals.reshape(128, 128, 128), cot,
    )
    grad_weight = gweight.reshape(64, 256).T * (1.0 / math.sqrt(64 * 4096))
    return out, gfeats, grad_weight


def solution(mesh):
    in_specs = (
        P("feat", "rows"),
        P(),
        P("rows", None),
        P("rows"),
        P("rows", None, None),
        P("rows", None),
        P("rows", None),
        P("rows", None, None, None),
        P("feat", "rows"),
    )
    out_specs = (P("feat", "rows"), P("feat", "rows"), P(None, "feat"))
    return jax.shard_map(
        on_device, mesh=mesh, in_specs=in_specs, out_specs=out_specs, check_vma=False
    )
```
